512 devices in a mesh: fsdp: 32 (over z, x_hi, core), dp: 16 (over y, x_lo).
Axes of the slice: x: 4 (x_hi: 2, x_lo: 2; x = x_hi * 2 + x_lo), y: 8, z: 8, core: 2. Of those that a mesh axis runs over, the one named last changes fastest.
Arguments:
- grad: bfloat16 [64, 1024, 1024], P(None, ('dp', 'fsdp')), may hold values from -64 to 64
- left_root: bfloat16 [64, 1024, 1024], P('fsdp', 'dp'), may hold values from -20 to 20, as said below
- right_root: bfloat16 [64, 1024, 1024], P('fsdp', 'dp'), may hold values from -20 to 20, as said below
- master: float32 [64, 1024, 1024], P('fsdp', 'dp'), may hold values from -6 to 6
- momentum: float32 [64, 1024, 1024], P('fsdp', 'dp'), may hold values from -6 to 6
- second: float32 [64, 1024, 1024], P('fsdp', 'dp'), may hold values from 0.25 to 4
Outputs:
- params: bfloat16 [64, 1024, 1024], P('fsdp')
- new_master: float32 [64, 1024, 1024], P('fsdp', 'dp')
- new_momentum: float32 [64, 1024, 1024], P('fsdp', 'dp')
- new_second: float32 [64, 1024, 1024], P('fsdp', 'dp')
The draws below stay inside these ranges and needn't reach their ends.
Inputs may be any that keep to these rules, and one draw needn't show every extreme that they name: `left_root`: each block is symmetric. `right_root`: each block is symmetric.
All inputs are finite; a program needn't handle non-finite values.
Results may differ from the reference program's by a relative error of at most 0.0075.
Values may be sent and summed in bfloat16 or wider, within the bound.
No kernel may reach another device: no remote copies, remote signals or barrier semaphores. Data moves between devices by JAX's collectives and lax.ppermute only.
A program may use at most 64 MiB of HBM per device.

```python
import math
import jax
import jax.numpy as jnp
from jax import lax

B = 1024
BLOCKS = 64


def symmetric_root(key, rise, spread):
    first_key, second_key = jax.random.split(key)
    position = jnp.arange(B, dtype=jnp.float32) / B
    diagonal = (rise ** position)[None, :] * jnp.exp(jax.random.uniform(first_key, (BLOCKS, B), jnp.float32) * math.log(spread))
    noise = jax.random.normal(second_key, (BLOCKS, B, B), jnp.float32)
    identity = jnp.eye(B, dtype=jnp.float32)
    coupling = (noise + jnp.swapaxes(noise, 1, 2)) * (0.45 / math.sqrt(2.0 * B)) * (1.0 - identity)
    half_root = jnp.sqrt(diagonal)
    matrix = half_root[:, :, None] * half_root[:, None, :] * (identity + coupling)
    return jnp.clip(matrix, -20.0, 20.0).astype(jnp.bfloat16)


def draw_left_root(key, part):
    key = jax.random.fold_in(key, 11)
    return symmetric_root(key, 3.0, 3.0)


def draw_right_root(key, part):
    key = jax.random.fold_in(key, 12)
    return symmetric_root(key, 3.0, 3.0)


def draw_grad(key, part):
    key = jax.random.fold_in(key, 7)
    row_key, column_key, noise_key = jax.random.split(key, 3)
    position = jnp.arange(B, dtype=jnp.float32) / B
    column_scale = jnp.exp(jax.random.uniform(column_key, (BLOCKS, 1, B), jnp.float32) * math.log(3.3))
    noise = jax.random.truncated_normal(noise_key, -4.0, 4.0, (BLOCKS, B, B), jnp.float32)
    row_scale = (3.0 ** position)[None, :, None] * jnp.exp(jax.random.uniform(row_key, (BLOCKS, B, 1), jnp.float32) * math.log(3.3))
    values = noise
    return jnp.clip(0.3 * values * row_scale * column_scale, -64.0, 64.0).astype(jnp.bfloat16)


def level_of(rng, shape, shards, least, high):
    factor_of = 1.0
    for dim, blocks in shards:
        steps = jax.random.uniform(jax.random.fold_in(jax.random.fold_in(rng, 6), dim), (blocks,), jnp.float32, least / len(shards), high / len(shards))
        factor_of = factor_of * jnp.repeat(jnp.exp(steps), shape[dim] // blocks).reshape((-1,) + (1,) * (len(shape) - 1 - dim))
    return factor_of


def gaussian(rng, extent, scale, bound, cuts=(), held_as=jnp.bfloat16):
    result = jax.random.normal(rng, extent, jnp.float32) * scale
    if len(cuts) > 0:
        result = level_of(rng, extent, cuts, -0.22, 0.18) * result
    return jnp.clip(result, min=-bound, max=bound).astype(held_as)


def setup_inputs(seed: int = 0) -> dict:
    streams_of = jax.random.split(jax.random.key(seed), 7)
    return {
        "grad": draw_grad(jax.random.fold_in(streams_of[6], 71), 0),
        "left_root": draw_left_root(jax.random.fold_in(streams_of[6], 71), 0),
        "right_root": draw_right_root(jax.random.fold_in(streams_of[6], 71), 0),
        "master": gaussian(streams_of[3], (BLOCKS, B, B), 1.0, 6.0, ((0, 32), (1, 16)), jnp.float32),
        "momentum": gaussian(streams_of[4], (BLOCKS, B, B), 1.0, 6.0, ((0, 32), (1, 16)), jnp.float32),
        "second": jnp.clip(jnp.exp(math.log(4.0) - 2.7725887 * jax.random.uniform(streams_of[5], (BLOCKS, B, B), jnp.float32) ** level_of(streams_of[5], (BLOCKS, B, B), ((0, 32), (1, 16)), -0.2, 0.2)), 0.25, 4.0),
    }


momentum_decay = 0.9
second_decay = 0.95
learn_rate = 0.05
adam_eps = 1e-08
norm_eps = 1e-06

def one_block(items):
    grad_block, left_block, right_block, master_block, momentum_block, second_block = items
    grad_float = grad_block.astype(jnp.float32)
    new_second = second_decay * second_block + (1.0 - second_decay) * grad_float * grad_float
    adam_step = grad_float / (jnp.sqrt(new_second) + adam_eps)
    left_grad = jnp.dot(left_block, grad_block, preferred_element_type=jnp.float32).astype(jnp.bfloat16)
    precond = jnp.dot(left_grad, right_block, preferred_element_type=jnp.float32)
    graft = jnp.sqrt(jnp.sum(adam_step * adam_step) / (jnp.sum(precond * precond) + norm_eps))
    new_momentum = momentum_decay * momentum_block + graft * precond
    new_master = master_block - learn_rate * new_momentum
    return (new_master.astype(jnp.bfloat16), new_master, new_momentum, new_second)

def reference(grad, left_root, right_root, master, momentum, second):
    results = lax.map(one_block, (grad, left_root, right_root, master, momentum, second))
    return (results[0], results[1], results[2], results[3])
```

```python
import jax
import jax.numpy as jnp
from jax import lax
from jax.experimental import pallas as pl
from jax.experimental.pallas import tpu as pltpu
from jax.sharding import Mesh, PartitionSpec as P

momentum_decay = 0.9
second_decay = 0.95
learn_rate = 0.05
adam_eps = 1e-08
norm_eps = 1e-06

Y = 8
OWNERS = ("z", "xh", "c")
GROUP = ("y", "xl")
SWAP = [(0, 1), (1, 0)]


def shift(step):
    return [(i, (i + step) % Y) for i in range(Y)]


def swap(x):
    return lax.ppermute(x, "xl", SWAP)


def ring(chunk):
    found = [(0, chunk)]
    ahead = behind = chunk
    for step in range(1, 5):
        ahead = lax.ppermute(ahead, "y", shift(1))
        found.append((-step, ahead))
        if step < 4:
            behind = lax.ppermute(behind, "y", shift(-1))
            found.append((step, behind))
    return found


def products_kernel(distances, y_ref, left_own, left_other, right, *refs):
    chunks = refs[: len(distances)]
    own, other, squares = refs[len(distances) :]
    rows = left_own.shape[0]
    depth = chunks[0].shape[0]
    y = y_ref[0]
    total = jnp.zeros((2 * rows, right.shape[0]), jnp.float32)
    for distance, chunk in zip(distances, chunks):
        at = pl.multiple_of(lax.rem(y + distance + Y, Y) * depth, depth)
        columns = jnp.concatenate(
            [left_own[:, pl.ds(at, depth)], left_other[:, pl.ds(at, depth)]], axis=0
        )
        total += jnp.dot(columns, chunk[...], preferred_element_type=jnp.float32)
    left_grad = total.astype(jnp.bfloat16)
    precond = jnp.dot(left_grad, right[...], preferred_element_type=jnp.float32)
    own[...] = precond[:rows]
    other[...] = precond[rows:]
    squares[...] = jnp.full(squares.shape, jnp.sum(precond * precond), jnp.float32)


def products(y, left_own, left_other, right, found):
    rows, width = left_own.shape
    vmem = pl.BlockSpec(memory_space=pltpu.VMEM)
    distances = [distance for distance, _ in found]

    def kernel(*refs):
        products_kernel(distances, *refs)

    return pl.pallas_call(
        kernel,
        out_shape=(
            jax.ShapeDtypeStruct((rows, width), jnp.float32),
            jax.ShapeDtypeStruct((rows, width), jnp.float32),
            jax.ShapeDtypeStruct((1, 128), jnp.float32),
        ),
        in_specs=[pl.BlockSpec(memory_space=pltpu.SMEM)] + [vmem] * (3 + len(found)),
        out_specs=(vmem, vmem, vmem),
        compiler_params=pltpu.CompilerParams(vmem_limit_bytes=24 * 1024 * 1024),
        cost_estimate=pl.CostEstimate(
            flops=8 * rows * width * width, bytes_accessed=6 * width * width, transcendentals=0
        ),
    )(y, left_own, left_other, right, *[chunk for _, chunk in found])


def on_device(grad, left_root, right_root, master, momentum, second):
    y = lax.axis_index("y")
    half = lax.axis_index("xl")
    rows = master.shape[1]
    width = master.shape[2]
    first = half == 0

    def pick(x, index):
        return lax.dynamic_index_in_dim(x, index, 0, keepdims=False)

    def ordered(own, other):
        return jnp.where(first, jnp.stack([own, other]), jnp.stack([other, own]))

    away = jnp.stack([pick(right_root, 1 - half), pick(left_root, 1 - half)])
    came = swap(away)
    right_pair = ordered(pick(right_root, half), came[0]).reshape(2 * rows, width)
    right = lax.all_gather(right_pair, "y", axis=0, tiled=True)

    spread = lax.all_to_all(grad, OWNERS + ("xl",), split_axis=0, concat_axis=1, tiled=True)
    pair = spread.reshape(-1, 2, grad.shape[1], width).swapaxes(0, 1).reshape(2 * rows, width)
    found = ring(pair)

    halves = pair.reshape(2, rows, width)
    other_grad = swap(pick(halves, 1 - half))
    owned = ordered(pick(halves, half), other_grad)
    grad_float = owned.astype(jnp.float32)
    new_second = second_decay * second + (1.0 - second_decay) * grad_float * grad_float
    adam_step = grad_float / (jnp.sqrt(new_second) + adam_eps)
    adam_squares = jnp.sum(adam_step * adam_step, axis=(1, 2))

    own, other, squares = products(y[None], pick(left_root, half), came[1], right, found)
    precond = ordered(own, swap(other))

    sums = jnp.concatenate([squares[:, :126], adam_squares[None, :]], axis=1)
    sums = jnp.broadcast_to(sums[None], (2 * Y, 1, 128))
    sums = lax.all_to_all(sums, GROUP, split_axis=0, concat_axis=0, tiled=True)
    sums = jnp.sum(sums.reshape(Y, 2, 128), axis=0)
    adam_total = sums[0, 126:] + sums[1, 126:]
    graft = jnp.sqrt(adam_total / (sums[:, 0] + norm_eps))

    new_momentum = momentum_decay * momentum + graft[:, None, None] * precond
    new_master = master - learn_rate * new_momentum

    rounded = new_master.astype(jnp.bfloat16)
    partner = swap(rounded)
    both = jnp.where(
        first,
        jnp.concatenate([rounded, partner], axis=1),
        jnp.concatenate([partner, rounded], axis=1),
    )
    params = jnp.zeros((2, Y, 2 * rows, width), jnp.bfloat16)
    for distance, chunk in ring(both):
        at = lax.rem(y + distance + Y, Y)
        params = lax.dynamic_update_slice(params, chunk[:, None], (0, at, 0, 0))
    params = params.reshape(2, 2 * Y * rows, width)
    return (params, new_master, new_momentum, new_second)


def solution(mesh):
    split = Mesh(mesh.devices.reshape(8, 2, 2, 8, 2), OWNERS + GROUP)
    state = P(OWNERS, GROUP, None)
    return jax.shard_map(
        on_device,
        mesh=split,
        in_specs=(P(None, GROUP + OWNERS, None),) + (state,) * 5,
        out_specs=(P(OWNERS, None, None), state, state, state),
        check_vma=False,
    )
```

```python
import jax
import jax.numpy as jnp
from jax import lax
from jax.experimental import pallas as pl
from jax.experimental.pallas import tpu as pltpu
from jax.sharding import Mesh, PartitionSpec as P

momentum_decay = 0.9
second_decay = 0.95
learn_rate = 0.05
adam_eps = 1e-08
norm_eps = 1e-06

Y = 8
OWNERS = ("z", "xh", "c")
GROUP = ("y", "xl")
SWAP = [(0, 1), (1, 0)]
VMEM = pl.BlockSpec(memory_space=pltpu.VMEM)
SMEM = pl.BlockSpec(memory_space=pltpu.SMEM)
PARAMS = pltpu.CompilerParams(vmem_limit_bytes=24 * 1024 * 1024)


def shift(step):
    return [(i, (i + step) % Y) for i in range(Y)]


def swap(x):
    return lax.ppermute(x, "xl", SWAP)


def ring(chunk):
    found = [(0, chunk)]
    ahead = behind = chunk
    for step in range(1, 5):
        ahead = lax.ppermute(ahead, "y", shift(1))
        found.append((-step, ahead))
        if step < 4:
            behind = lax.ppermute(behind, "y", shift(-1))
            found.append((step, behind))
    return found


def left_kernel(distances, place, left_own, left_other, *refs):
    chunks, out = refs[:-1], refs[-1]
    rows = left_own.shape[0]
    depth = chunks[0].shape[0]
    total = jnp.zeros((2 * rows, out.shape[1]), jnp.float32)
    for distance, chunk in zip(distances, chunks):
        at = pl.multiple_of(lax.rem(place[0] + distance + Y, Y) * depth, depth)
        columns = jnp.concatenate(
            [left_own[:, pl.ds(at, depth)], left_other[:, pl.ds(at, depth)]], axis=0
        )
        total += jnp.dot(columns, chunk[...], preferred_element_type=jnp.float32)
    rounded = total.astype(jnp.bfloat16)
    half = place[1]
    out[pl.ds(pl.multiple_of(half * rows, rows), rows), :] = rounded[:rows]
    out[pl.ds(pl.multiple_of((1 - half) * rows, rows), rows), :] = rounded[rows:]


def right_kernel(place, adam, mine, theirs, right, out, sums):
    depth = right.shape[0] * right.shape[2]
    half = place[1]
    squares = []
    for block in range(2):
        left_grad = jnp.where(half == block, mine[...], theirs[...])
        columns = right[:, block].reshape(depth, right.shape[3])
        part = lax.dot_general(
            left_grad, columns, (((1,), (1,)), ((), ())), preferred_element_type=jnp.float32
        )
        out[block] = part.astype(jnp.bfloat16)
        squares.append(jnp.sum(part * part))
    row = lax.broadcasted_iota(jnp.int32, (8, 128), 0)
    values = jnp.where(row < 2, jnp.where(row == 0, squares[0], squares[1]), jnp.where(row == 2, adam[0], adam[1]))
    for i in range(sums.shape[0]):
        sums[i] = values


def update_kernel(place, sums, mine, theirs, base_own, base_other, master, momentum, params, new_master, new_momentum, precond):
    rows, width = master.shape[1:]
    half = place[1]
    total = jnp.sum(sums[...], axis=0)
    own = pl.ds(pl.multiple_of(half * rows, rows), rows)
    other = pl.ds(pl.multiple_of((1 - half) * rows, rows), rows)
    low = lax.broadcasted_iota(jnp.int32, (2 * rows, 128), 1) < 64
    for block in range(2):
        graft = jnp.sqrt(total[2 + block : 3 + block] / (total[block : block + 1] + norm_eps))
        for i in range(Y // 2):
            cut = slice(i * 128, (i + 1) * 128)
            a = mine[block, :, cut].astype(jnp.float32)
            b = theirs[block, :, cut].astype(jnp.float32)
            first = jnp.where(half == 0, a, b)
            second = jnp.where(half == 0, b, a)
            even = jnp.where(low, first, pltpu.roll(second, 64, 1))
            odd = jnp.where(low, pltpu.roll(first, 64, 1), second)
            precond[:, 2 * i * 128 : (2 * i + 1) * 128] = graft * even
            precond[:, (2 * i + 1) * 128 : (2 * i + 2) * 128] = graft * odd
        ours = precond[own, :]
        moved = momentum_decay * momentum[block] + ours
        new_momentum[block] = moved
        new_master[block] = master[block] - learn_rate * moved
        params[block, own, :] = (base_own[block] - learn_rate * ours).astype(jnp.bfloat16)
        params[block, other, :] = (base_other[block] - learn_rate * precond[other, :]).astype(jnp.bfloat16)


def on_device(grad, left_root, right_root, master, momentum, second):
    y = lax.axis_index("y")
    half = lax.axis_index("xl")
    place = jnp.stack([y, half])
    _, rows, width = master.shape
    first = half == 0
    f32, bf16 = jnp.float32, jnp.bfloat16

    def pick(x, index):
        return lax.dynamic_index_in_dim(x, index, 0, keepdims=False)

    right = lax.all_gather(right_root, "y", axis=0, tiled=False)

    spread = lax.all_to_all(grad, OWNERS + ("xl",), split_axis=0, concat_axis=1, tiled=True)
    pair = spread.reshape(-1, 2, grad.shape[1], width).swapaxes(0, 1).reshape(2 * rows, width)
    found = ring(pair)

    left_other = swap(pick(left_root, 1 - half))
    base_own = master - (learn_rate * momentum_decay) * momentum
    base_other = swap(base_own)

    halves = pair.reshape(2, rows, width)
    other_grad = swap(pick(halves, 1 - half))
    own_grad = pick(halves, half)
    owned = jnp.where(first, jnp.stack([own_grad, other_grad]), jnp.stack([other_grad, own_grad]))
    grad_float = owned.astype(f32)
    new_second = second_decay * second + (1.0 - second_decay) * grad_float * grad_float
    adam_step = grad_float / (jnp.sqrt(new_second) + adam_eps)
    adam_squares = jnp.sum(adam_step * adam_step, axis=(1, 2))

    distances = [distance for distance, _ in found]
    left_grad = pl.pallas_call(
        lambda *refs: left_kernel(distances, *refs),
        out_shape=jax.ShapeDtypeStruct((2 * rows, width), bf16),
        in_specs=[SMEM] + [VMEM] * (2 + len(found)),
        out_specs=VMEM,
        compiler_params=PARAMS,
        cost_estimate=pl.CostEstimate(
            flops=4 * rows * width * width, bytes_accessed=3 * width * width, transcendentals=0
        ),
    )(place, pick(left_root, half), left_other, *[chunk for _, chunk in found])
    left_grad_other = swap(left_grad)

    part, sums = pl.pallas_call(
        right_kernel,
        out_shape=(
            jax.ShapeDtypeStruct((2, 2 * rows, width // 2), bf16),
            jax.ShapeDtypeStruct((2 * Y, 8, 128), f32),
        ),
        in_specs=[SMEM, SMEM] + [VMEM] * 3,
        out_specs=(VMEM, VMEM),
        compiler_params=PARAMS,
        cost_estimate=pl.CostEstimate(
            flops=4 * rows * width * width, bytes_accessed=3 * width * width, transcendentals=0
        ),
    )(place, adam_squares, left_grad, left_grad_other, right)
    part_other = swap(part)
    sums = lax.all_to_all(sums, GROUP, split_axis=0, concat_axis=0, tiled=True)

    both, new_master, new_momentum = pl.pallas_call(
        update_kernel,
        out_shape=(
            jax.ShapeDtypeStruct((2, 2 * rows, width), bf16),
            jax.ShapeDtypeStruct(master.shape, f32),
            jax.ShapeDtypeStruct(master.shape, f32),
        ),
        in_specs=[SMEM] + [VMEM] * 7,
        out_specs=(VMEM, VMEM, VMEM),
        scratch_shapes=[pltpu.VMEM((2 * rows, width), f32)],
        compiler_params=PARAMS,
        cost_estimate=pl.CostEstimate(
            flops=16 * rows * width, bytes_accessed=60 * rows * width, transcendentals=0
        ),
    )(place, sums, part, part_other, base_own, base_other, master, momentum)

    params = jnp.zeros((2, Y, 2 * rows, width), bf16)
    ahead = behind = both

    def put(params, chunk, block, distance):
        at = lax.rem(y + distance + Y, Y)
        return lax.dynamic_update_slice(params, chunk[:, None], (block, at, 0, 0))

    params = put(params, both, 0, 0)
    for step in range(1, 4):
        ahead = lax.ppermute(ahead, "y", shift(1))
        behind = lax.ppermute(behind, "y", shift(-1))
        params = put(params, ahead, 0, -step)
        params = put(params, behind, 0, step)
    params = put(params, lax.ppermute(ahead[:1], "y", shift(1)), 0, 4)
    params = put(params, lax.ppermute(behind[1:], "y", shift(-1)), 1, 4)
    params = params.reshape(2, 2 * Y * rows, width)
    return (params, new_master, new_momentum, new_second)


def solution(mesh):
    split = Mesh(mesh.devices.reshape(8, 2, 2, 8, 2), OWNERS + GROUP)
    state = P(OWNERS, GROUP, None)
    return jax.shard_map(
        on_device,
        mesh=split,
        in_specs=(P(None, GROUP + OWNERS, None),) + (state,) * 5,
        out_specs=(P(OWNERS, None, None), state, state, state),
        check_vma=False,
    )
```

```python
import jax
import jax.numpy as jnp
from jax import lax
from jax.experimental import pallas as pl
from jax.experimental.pallas import tpu as pltpu
from jax.sharding import Mesh, PartitionSpec as P

momentum_decay = 0.9
second_decay = 0.95
learn_rate = 0.05
adam_eps = 1e-08
norm_eps = 1e-06

Y = 8
OWNERS = ("z", "xh", "c")
GROUP = ("y", "xl")
SWAP = [(0, 1), (1, 0)]
VMEM = pl.BlockSpec(memory_space=pltpu.VMEM)
PARAMS = pltpu.CompilerParams(vmem_limit_bytes=24 * 1024 * 1024)


def swap(x):
    return lax.ppermute(x, "xl", SWAP)


def hop(x, way):
    pairs = [(c * Y + i, c * Y + (i + (way if c == 0 else -way)) % Y) for c in range(2) for i in range(Y)]
    return lax.ppermute(x, ("c", "y"), pairs)


def after(x, *others):
    return lax.optimization_barrier((x, *others))


def left_kernel(distances, place, left_own, left_other, *refs):
    chunks, out = refs[:-1], refs[-1]
    rows = left_own.shape[1]
    depth = chunks[0].shape[0]
    half = place[1]
    total = jnp.zeros((2 * rows, out.shape[1]), jnp.float32)
    for distance, chunk in zip(distances, chunks):
        at = lax.rem(place[0] + place[2] * distance + Y, Y)
        at = pl.multiple_of(at * depth, depth)
        columns = jnp.concatenate(
            [left_own[half, :, pl.ds(at, depth)], left_other[half, :, pl.ds(at, depth)]], axis=0
        )
        total += jnp.dot(columns, chunk[...], preferred_element_type=jnp.float32)
    rounded = total.astype(jnp.bfloat16)
    out[pl.ds(pl.multiple_of(half * rows, rows), rows), :] = rounded[:rows]
    out[pl.ds(pl.multiple_of((1 - half) * rows, rows), rows), :] = rounded[rows:]


def adam_kernel(place, mine, theirs, second, new_second, squares):
    rows = second.shape[1]
    half = place[1]
    own = pl.ds(pl.multiple_of(half * rows, rows), rows)
    ours, others = mine[own, :], theirs[own, :]
    for block in range(2):
        grad = jnp.where(half == block, ours, others).astype(jnp.float32)
        moment = second_decay * second[block] + (1.0 - second_decay) * grad * grad
        new_second[block] = moment
        step = grad / (jnp.sqrt(moment) + adam_eps)
        squares[block] = jnp.full(squares.shape[1:], jnp.sum(step * step), jnp.float32)


def right_kernel(place, mine, theirs, right, adam, out, sums):
    depth = right.shape[0] * right.shape[2]
    half = place[1]
    squares = []
    for block in range(2):
        left_grad = jnp.where(half == block, mine[...], theirs[...])
        columns = right[:, block].reshape(depth, right.shape[3])
        part = lax.dot_general(
            left_grad, columns, (((1,), (1,)), ((), ())), preferred_element_type=jnp.float32
        )
        out[block] = part.astype(jnp.bfloat16)
        squares.append(jnp.sum(part * part))
    row = lax.broadcasted_iota(jnp.int32, (8, 128), 0)
    values = jnp.where(row < 2, jnp.where(row == 0, squares[0], squares[1]), jnp.where(row == 2, adam[0][:1], adam[1][:1]))
    for i in range(sums.shape[0]):
        sums[i] = values


def update_kernel(place, sums, mine, theirs, base_own, base_other, master, momentum, params, new_master, new_momentum, precond):
    rows, width = master.shape[1:]
    half = place[1]
    total = jnp.sum(sums[...], axis=0)
    own = pl.ds(pl.multiple_of(half * rows, rows), rows)
    other = pl.ds(pl.multiple_of((1 - half) * rows, rows), rows)
    low = lax.broadcasted_iota(jnp.int32, (2 * rows, 128), 1) < 64
    for block in range(2):
        graft = jnp.sqrt(total[2 + block : 3 + block] / (total[block : block + 1] + norm_eps))
        for i in range(Y // 2):
            cut = slice(i * 128, (i + 1) * 128)
            a = mine[block, :, cut].astype(jnp.float32)
            b = theirs[block, :, cut].astype(jnp.float32)
            first = jnp.where(half == 0, a, b)
            second = jnp.where(half == 0, b, a)
            even = jnp.where(low, first, pltpu.roll(second, 64, 1))
            odd = jnp.where(low, pltpu.roll(first, 64, 1), second)
            precond[:, 2 * i * 128 : (2 * i + 1) * 128] = graft * even
            precond[:, (2 * i + 1) * 128 : (2 * i + 2) * 128] = graft * odd
        ours = precond[own, :]
        moved = momentum_decay * momentum[block] + ours
        new_momentum[block] = moved
        new_master[block] = master[block] - learn_rate * moved
        params[block, own, :] = (base_own[block] - learn_rate * ours).astype(jnp.bfloat16)
        params[block, other, :] = (base_other[block] - learn_rate * precond[other, :]).astype(jnp.bfloat16)


def call(kernel, out_shape, operands, flops=0, scratch_shapes=()):
    leaves = jax.tree.leaves(out_shape)
    moved = sum(x.size * x.dtype.itemsize for x in (*operands, *leaves))
    return pl.pallas_call(
        kernel,
        out_shape=out_shape,
        in_specs=[pl.BlockSpec(memory_space=pltpu.SMEM)] + [VMEM] * (len(operands) - 1),
        out_specs=jax.tree.map(lambda _: VMEM, out_shape),
        scratch_shapes=scratch_shapes,
        compiler_params=PARAMS,
        cost_estimate=pl.CostEstimate(flops=flops, bytes_accessed=moved, transcendentals=0),
    )(*operands)


def on_device(grad, left_root, right_root, master, momentum, second):
    y = lax.axis_index("y")
    half = lax.axis_index("xl")
    sign = 1 - 2 * lax.axis_index("c")
    place = jnp.stack([y, half, sign])
    _, rows, width = master.shape
    shape = jax.ShapeDtypeStruct
    f32, bf16 = jnp.float32, jnp.bfloat16

    right = lax.all_gather(right_root, "y", axis=0, tiled=False)

    spread = lax.all_to_all(grad, OWNERS + ("xl",), split_axis=0, concat_axis=1, tiled=True)
    pair = spread.reshape(-1, 2, grad.shape[1], width).swapaxes(0, 1).reshape(2 * rows, width)

    up1, down1 = hop(pair, 1), hop(pair, -1)
    base = master - (learn_rate * momentum_decay) * momentum
    up1, left, base = after(up1, left_root, base)
    left_other, base_other, pair_other = swap(left), swap(base), swap(pair)
    up2, down2 = hop(up1, 1), hop(down1, -1)
    up2, left_other = after(up2, left_other)
    up3, down3 = hop(up2, 1), hop(down2, -1)
    up3, down3, pair_other, base_other, right = after(up3, down3, pair_other, base_other, right)
    new_second, squares = call(
        adam_kernel,
        (shape(second.shape, f32), shape((2, 8, 128), f32)),
        (place, pair, pair_other, second),
    )
    up4 = hop(up3, 1)
    up4, squares = after(up4, squares)
    chunks = (pair, up1, down1, up2, down2, up3, down3, up4)
    distances = (0, -1, 1, -2, 2, -3, 3, -4)

    flops = 4 * rows * width * width
    left_grad = call(
        lambda *refs: left_kernel(distances, *refs),
        shape((2 * rows, width), bf16),
        (place, left_root, left_other, *chunks),
        flops,
    )
    part, sums = call(
        right_kernel,
        (shape((2, 2 * rows, width // 2), bf16), shape((2 * Y, 8, 128), f32)),
        (place, left_grad, swap(left_grad), right, squares),
        flops,
    )
    part_other = swap(part)
    sums = lax.all_to_all(sums, GROUP, split_axis=0, concat_axis=0, tiled=True)

    both, new_master, new_momentum = call(
        update_kernel,
        (shape((2, 2 * rows, width), bf16), shape(master.shape, f32), shape(master.shape, f32)),
        (place, sums, part, part_other, base, base_other, master, momentum),
        scratch_shapes=[pltpu.VMEM((2 * rows, width), f32)],
    )

    params = jnp.zeros((2, Y, 2 * rows, width), bf16)

    def put(params, chunk, block, distance):
        at = lax.rem(y + sign * distance + Y, Y)
        return lax.dynamic_update_slice(params, chunk[:, None], (block, at, 0, 0))

    params = put(params, both, 0, 0)
    up = down = both
    for step in range(1, 4):
        up, down = hop(up, 1), hop(down, -1)
        params = put(params, up, 0, -step)
        params = put(params, down, 0, step)
    params = put(params, hop(up[:1], 1), 0, 4)
    params = put(params, hop(down[1:], -1), 1, 4)
    params = params.reshape(2, 2 * Y * rows, width)
    return (params, new_master, new_momentum, new_second)


def solution(mesh):
    split = Mesh(mesh.devices.reshape(8, 2, 2, 8, 2), OWNERS + GROUP)
    state = P(OWNERS, GROUP, None)
    return jax.shard_map(
        on_device,
        mesh=split,
        in_specs=(P(None, GROUP + OWNERS, None),) + (state,) * 5,
        out_specs=(P(OWNERS, None, None), state, state, state),
        check_vma=False,
    )
```

```python
import jax
import jax.numpy as jnp
from jax import lax
from jax.experimental import pallas as pl
from jax.experimental.pallas import tpu as pltpu
from jax.sharding import Mesh, PartitionSpec as P

momentum_decay = 0.9
second_decay = 0.95
learn_rate = 0.05
adam_eps = 1e-08
norm_eps = 1e-06

Y = 8
OWNERS = ("z", "xh", "c")
GROUP = ("y", "xl")
SWAP = [(0, 1), (1, 0)]
VMEM = pl.BlockSpec(memory_space=pltpu.VMEM)
SMEM = pl.BlockSpec(memory_space=pltpu.SMEM)
ANY = pl.BlockSpec(memory_space=pl.ANY)
PARAMS = pltpu.CompilerParams(vmem_limit_bytes=12 * 1024 * 1024)


def swap(x):
    return lax.ppermute(x, "xl", SWAP)


def hop(x, way):
    return lax.ppermute(x, "y", [(i, (i + way) % Y) for i in range(Y)])


def adam_kernel(place, mine, theirs, second, *refs):
    new_second, squares = refs[-2:]
    rows = second.shape[1]
    half = place[1]
    ours = mine[pl.ds(pl.multiple_of(half * rows, rows), rows), :]
    others = theirs[pl.ds(pl.multiple_of(half * rows, rows), rows), :]
    for block in range(2):
        grad = jnp.where(half == block, ours, others).astype(jnp.float32)
        moment = second_decay * second[block] + (1.0 - second_decay) * grad * grad
        new_second[block] = moment
        step = grad / (jnp.sqrt(moment) + adam_eps)
        squares[block] = jnp.full(squares.shape[1:], jnp.sum(step * step), jnp.float32)


def left_kernel(distances, place, left_own, swapped, *refs):
    chunks, out = refs[: len(distances)], refs[-1]
    rows = left_own.shape[1]
    depth = chunks[0].shape[0]
    half = place[1]
    total = jnp.zeros((2 * rows, out.shape[1]), jnp.float32)
    for distance, chunk in zip(distances, chunks):
        at = pl.multiple_of(lax.rem(place[0] + distance + Y, Y) * depth, depth)
        columns = jnp.concatenate(
            [left_own[half, :, pl.ds(at, depth)], swapped[:rows, pl.ds(at, depth)]], axis=0
        )
        total += jnp.dot(columns, chunk[...], preferred_element_type=jnp.float32)
    rounded = total.astype(jnp.bfloat16)
    out[pl.ds(pl.multiple_of(half * rows, rows), rows), :] = rounded[:rows]
    out[pl.ds(pl.multiple_of((1 - half) * rows, rows), rows), :] = rounded[rows:]


def right_kernel(place, left_grads, adam, right, out, sums):
    depth = right.shape[0] * right.shape[2]
    squares = []
    for block in range(2):
        columns = right[:, block].reshape(depth, right.shape[3])
        part = lax.dot_general(
            left_grads[block], columns, (((1,), (1,)), ((), ())), preferred_element_type=jnp.float32
        )
        out[block] = part.astype(jnp.bfloat16)
        squares.append(jnp.sum(part * part))
    row = lax.broadcasted_iota(jnp.int32, (8, 128), 0)
    values = jnp.where(
        row < 2, jnp.where(row == 0, squares[0], squares[1]), jnp.where(row == 2, adam[0][:1], adam[1][:1])
    )
    for i in range(sums.shape[0]):
        sums[i] = values


def grafted(place, sums, mine, theirs, block, precond):
    half = place[1]
    total = jnp.sum(sums[...], axis=0)
    graft = jnp.sqrt(total[2 + block : 3 + block] / (total[block : block + 1] + norm_eps))
    low = lax.broadcasted_iota(jnp.int32, (precond.shape[0], 128), 1) < 64
    for i in range(Y // 2):
        cut = slice(i * 128, (i + 1) * 128)
        a = mine[block, :, cut].astype(jnp.float32)
        b = theirs[block, :, cut].astype(jnp.float32)
        first = jnp.where(half == 0, a, b)
        second = jnp.where(half == 0, b, a)
        even = jnp.where(low, first, pltpu.roll(second, 64, 1))
        odd = jnp.where(low, pltpu.roll(first, 64, 1), second)
        precond[:, 2 * i * 128 : (2 * i + 1) * 128] = graft * even
        precond[:, (2 * i + 1) * 128 : (2 * i + 2) * 128] = graft * odd


def update_kernel(
    place, sums, mine, theirs, base, swapped, master, momentum, params, new_master, new_momentum, precond
):
    rows = master.shape[1]
    own = pl.ds(pl.multiple_of(place[1] * rows, rows), rows)
    other = pl.ds(pl.multiple_of((1 - place[1]) * rows, rows), rows)
    for block in range(2):
        grafted(place, sums, mine, theirs, block, precond)
        ours = precond[own, :]
        params[block, own, :] = (base[block] - learn_rate * ours).astype(jnp.bfloat16)
        high = swapped[(1 + block) * rows : (2 + block) * rows, :].astype(jnp.float32)
        low = swapped[(3 + block) * rows : (4 + block) * rows, :].astype(jnp.float32)
        params[block, other, :] = (high + low - learn_rate * precond[other, :]).astype(jnp.bfloat16)
        moved = momentum_decay * momentum[block] + ours
        new_momentum[block] = moved
        new_master[block] = master[block] - learn_rate * moved


def call(kernel, out_shape, operands, flops=0, ready=(), through=None, scratch_shapes=()):
    moved = sum(x.size * x.dtype.itemsize for x in operands)
    in_specs = [SMEM] + [VMEM] * (len(operands) - 1) + [ANY] * len(ready)
    operands, out_shape = tuple(operands) + tuple(ready), tuple(out_shape)
    out_specs = [VMEM] * len(out_shape)
    aliases = {}
    if through is not None:
        aliases = {len(operands): len(out_shape)}
        operands += (through,)
        out_shape += (jax.ShapeDtypeStruct(through.shape, through.dtype),)
        in_specs.append(ANY)
        out_specs.append(ANY)
    return pl.pallas_call(
        kernel,
        out_shape=out_shape,
        in_specs=in_specs,
        out_specs=tuple(out_specs),
        scratch_shapes=scratch_shapes,
        input_output_aliases=aliases,
        compiler_params=PARAMS,
        cost_estimate=pl.CostEstimate(flops=flops, bytes_accessed=2 * moved, transcendentals=0),
    )(*operands)


def on_device(grad, left_root, right_root, master, momentum, second):
    place = jnp.stack([lax.axis_index("y"), lax.axis_index("xl")])
    _, rows, width = master.shape
    shape = jax.ShapeDtypeStruct
    f32, bf16 = jnp.float32, jnp.bfloat16

    right = lax.all_gather(right_root, "y", axis=0, tiled=False)

    value = master - (learn_rate * momentum_decay) * momentum
    high = value.astype(bf16)
    low = (value - high.astype(f32)).astype(bf16)
    base = high.astype(f32) + low.astype(f32)
    left_away = jnp.where(place[1] == 0, left_root[1], left_root[0])
    swapped = swap(jnp.concatenate([left_away[None], high, low]).reshape(5 * rows, width))

    spread = lax.all_to_all(grad, OWNERS + ("xl",), split_axis=0, concat_axis=1, tiled=True)
    pair = spread.reshape(-1, 2, grad.shape[1], width).swapaxes(0, 1).reshape(2 * rows, width)

    up1, down1 = hop(pair, 1), hop(pair, -1)
    up2, down2 = hop(up1, 1), hop(down1, -1)
    up3, down3 = hop(up2, 1), hop(down2, -1)
    up4 = hop(up3, 1)
    chunks = (pair, up1, down1, up2, down2, up3, down3, up4)
    distances = (0, -1, 1, -2, 2, -3, 3, -4)
    new_second, squares = call(
        adam_kernel,
        (shape(second.shape, f32), shape((2, 8, 128), f32)),
        (place, pair, swap(pair), second),
        ready=(right[0, 0, :16, :128],),
    )

    flops = 4 * rows * width * width
    (left_grad,) = call(
        lambda *refs: left_kernel(distances, *refs),
        (shape((2 * rows, width), bf16),),
        (place, left_root, swapped, *chunks),
        flops,
        ready=(squares,),
    )
    part, sums = call(
        right_kernel,
        (shape((2, 2 * rows, width // 2), bf16), shape((2 * Y, 8, 128), f32)),
        (place, lax.all_gather(left_grad, "xl", axis=0, tiled=False), squares, right),
        flops,
    )
    part_other = swap(part)
    sums = lax.all_to_all(sums, GROUP, split_axis=0, concat_axis=0, tiled=True)

    both, new_master, new_momentum = call(
        update_kernel,
        (shape((2, 2 * rows, width), bf16), shape(master.shape, f32), shape(master.shape, f32)),
        (place, sums, part, part_other, base, swapped, master, momentum),
        scratch_shapes=[pltpu.VMEM((2 * rows, width), f32)],
    )

    params = jnp.zeros((2, Y, 2 * rows, width), bf16)

    def put(params, chunk, block, distance):
        at = lax.rem(place[0] + distance + Y, Y)
        return lax.dynamic_update_slice(params, chunk[:, None], (block, at, 0, 0))

    params = put(params, both, 0, 0)
    up = down = both
    for step in range(1, 4):
        up, down = hop(up, 1), hop(down, -1)
        params = put(params, up, 0, -step)
        params = put(params, down, 0, step)
    params = put(params, hop(up[:1], 1), 0, 4)
    params = put(params, hop(down[1:], -1), 1, 4)
    params = params.reshape(2, 2 * Y * rows, width)
    return (params, new_master, new_momentum, new_second)


def solution(mesh):
    split = Mesh(mesh.devices.reshape(8, 2, 2, 8, 2), OWNERS + GROUP)
    state = P(OWNERS, GROUP, None)
    return jax.shard_map(
        on_device,
        mesh=split,
        in_specs=(P(None, GROUP + OWNERS, None),) + (state,) * 5,
        out_specs=(P(OWNERS, None, None), state, state, state),
        check_vma=False,
    )
```

```python
import jax
import jax.numpy as jnp
from jax import lax
from jax.experimental import pallas as pl
from jax.experimental.pallas import tpu as pltpu
from jax.sharding import Mesh, PartitionSpec as P

momentum_decay = 0.9
second_decay = 0.95
learn_rate = 0.05
adam_eps = 1e-08
norm_eps = 1e-06

Y = 8
OWNERS = ("z", "xh", "c")
GROUP = ("y", "xl")
SWAP = [(0, 1), (1, 0)]
VMEM = pl.BlockSpec(memory_space=pltpu.VMEM)
SMEM = pl.BlockSpec(memory_space=pltpu.SMEM)
ANY = pl.BlockSpec(memory_space=pl.ANY)
PARAMS = pltpu.CompilerParams(vmem_limit_bytes=12 * 1024 * 1024)


def swap(x):
    return lax.ppermute(x, "xl", SWAP)


def hop(x, way):
    return lax.ppermute(x, "y", [(i, (i + way) % Y) for i in range(Y)])


def adam_kernel(place, mine, theirs, second, *refs):
    new_second, squares = refs[-2:]
    rows = second.shape[1]
    half = place[1]
    ours = mine[pl.ds(pl.multiple_of(half * rows, rows), rows), :]
    others = theirs[pl.ds(pl.multiple_of(half * rows, rows), rows), :]
    for block in range(2):
        grad = jnp.where(half == block, ours, others).astype(jnp.float32)
        moment = second_decay * second[block] + (1.0 - second_decay) * grad * grad
        new_second[block] = moment
        step = grad / (jnp.sqrt(moment) + adam_eps)
        squares[block] = jnp.full(squares.shape[1:], jnp.sum(step * step), jnp.float32)


def left_kernel(distances, place, left_own, swapped, *refs):
    chunks, out = refs[: len(distances)], refs[-1]
    rows = left_own.shape[1]
    depth = chunks[0].shape[0]
    half = place[1]
    total = jnp.zeros((2 * rows, out.shape[1]), jnp.float32)
    for distance, chunk in zip(distances, chunks):
        at = pl.multiple_of(lax.rem(place[0] + distance + Y, Y) * depth, depth)
        columns = jnp.concatenate(
            [left_own[half, :, pl.ds(at, depth)], swapped[:rows, pl.ds(at, depth)]], axis=0
        )
        total += jnp.dot(columns, chunk[...], preferred_element_type=jnp.float32)
    rounded = total.astype(jnp.bfloat16)
    out[pl.ds(pl.multiple_of(half * rows, rows), rows), :] = rounded[:rows]
    out[pl.ds(pl.multiple_of((1 - half) * rows, rows), rows), :] = rounded[rows:]


def right_kernel(place, left_grads, adam, right, out, sums):
    depth = right.shape[0] * right.shape[2]
    squares = []
    for block in range(2):
        columns = right[:, block].reshape(depth, right.shape[3])
        part = lax.dot_general(
            left_grads[block], columns, (((1,), (1,)), ((), ())), preferred_element_type=jnp.float32
        )
        out[block] = part.astype(jnp.bfloat16)
        squares.append(jnp.sum(part * part))
    row = lax.broadcasted_iota(jnp.int32, (8, 128), 0)
    values = jnp.where(
        row < 2, jnp.where(row == 0, squares[0], squares[1]), jnp.where(row == 2, adam[0][:1], adam[1][:1])
    )
    sums[...] = values


def pair_sums_kernel(place, both, part, out, handed):
    for i in range(out.shape[0]):
        out[i] = both[0] + both[1]


def grafted(place, sums, mine, theirs, block, precond):
    half = place[1]
    total = jnp.sum(sums[...], axis=0)
    graft = jnp.sqrt(total[2 + block : 3 + block] / (total[block : block + 1] + norm_eps))
    low = lax.broadcasted_iota(jnp.int32, (precond.shape[0], 128), 1) < 64
    for i in range(Y // 2):
        cut = slice(i * 128, (i + 1) * 128)
        a = mine[block, :, cut].astype(jnp.float32)
        b = theirs[block, :, cut].astype(jnp.float32)
        first = jnp.where(half == 0, a, b)
        second = jnp.where(half == 0, b, a)
        even = jnp.where(low, first, pltpu.roll(second, 64, 1))
        odd = jnp.where(low, pltpu.roll(first, 64, 1), second)
        precond[:, 2 * i * 128 : (2 * i + 1) * 128] = graft * even
        precond[:, (2 * i + 1) * 128 : (2 * i + 2) * 128] = graft * odd


def update_kernel(
    place, sums, mine, theirs, base, swapped, master, momentum, params, new_master, new_momentum, precond
):
    rows = master.shape[1]
    own = pl.ds(pl.multiple_of(place[1] * rows, rows), rows)
    other = pl.ds(pl.multiple_of((1 - place[1]) * rows, rows), rows)
    for block in range(2):
        grafted(place, sums, mine, theirs, block, precond)
        ours = precond[own, :]
        params[block, own, :] = (base[block] - learn_rate * ours).astype(jnp.bfloat16)
        high = swapped[(1 + block) * rows : (2 + block) * rows, :].astype(jnp.float32)
        low = swapped[(3 + block) * rows : (4 + block) * rows, :].astype(jnp.float32)
        params[block, other, :] = (high + low - learn_rate * precond[other, :]).astype(jnp.bfloat16)
        moved = momentum_decay * momentum[block] + ours
        new_momentum[block] = moved
        new_master[block] = master[block] - learn_rate * moved


def call(kernel, out_shape, operands, flops=0, ready=(), through=None, scratch_shapes=()):
    moved = sum(x.size * x.dtype.itemsize for x in operands)
    in_specs = [SMEM] + [VMEM] * (len(operands) - 1) + [ANY] * len(ready)
    operands, out_shape = tuple(operands) + tuple(ready), tuple(out_shape)
    out_specs = [VMEM] * len(out_shape)
    aliases = {}
    if through is not None:
        aliases = {len(operands): len(out_shape)}
        operands += (through,)
        out_shape += (jax.ShapeDtypeStruct(through.shape, through.dtype),)
        in_specs.append(ANY)
        out_specs.append(ANY)
    return pl.pallas_call(
        kernel,
        out_shape=out_shape,
        in_specs=in_specs,
        out_specs=tuple(out_specs),
        scratch_shapes=scratch_shapes,
        input_output_aliases=aliases,
        compiler_params=PARAMS,
        cost_estimate=pl.CostEstimate(flops=flops, bytes_accessed=2 * moved, transcendentals=0),
    )(*operands)


def later(place, x, *ready):
    return call(lambda *refs: None, (), (place,), ready=ready, through=x)[0]


def on_device(grad, left_root, right_root, master, momentum, second):
    place = jnp.stack([lax.axis_index("y"), lax.axis_index("xl")])
    _, rows, width = master.shape
    shape = jax.ShapeDtypeStruct
    f32, bf16 = jnp.float32, jnp.bfloat16

    right = lax.all_gather(right_root, "y", axis=0, tiled=False)

    value = master - (learn_rate * momentum_decay) * momentum
    high = value.astype(bf16)
    low = (value - high.astype(f32)).astype(bf16)
    base = high.astype(f32) + low.astype(f32)
    left_away = jnp.where(place[1] == 0, left_root[1], left_root[0])
    away = jnp.concatenate([left_away[None], high, low]).reshape(5 * rows, width)

    spread = lax.all_to_all(grad, OWNERS + ("xl",), split_axis=0, concat_axis=1, tiled=True)
    pair = spread.reshape(-1, 2, grad.shape[1], width).swapaxes(0, 1).reshape(2 * rows, width)

    pair = later(place, pair, away, base)
    up1, down1 = hop(pair, 1), hop(pair, -1)
    swapped = swap(away)
    down1 = later(place, down1, swapped)
    up2, down2 = hop(up1, 1), hop(down1, -1)
    up3, down3 = hop(up2, 1), hop(down2, -1)
    up4 = hop(up3, 1)
    chunks = (pair, up1, down1, up2, down2, up3, down3, up4)
    distances = (0, -1, 1, -2, 2, -3, 3, -4)
    new_second, squares = call(
        adam_kernel,
        (shape(second.shape, f32), shape((2, 8, 128), f32)),
        (place, pair, swap(pair), second),
        ready=(right[0, 0, :16, :128],),
    )

    flops = 4 * rows * width * width
    (left_grad,) = call(
        lambda *refs: left_kernel(distances, *refs),
        (shape((2 * rows, width), bf16),),
        (place, left_root, swapped, *chunks),
        flops,
        ready=(squares,),
    )
    part, sums = call(
        right_kernel,
        (shape((2, 2 * rows, width // 2), bf16), shape((8, 128), f32)),
        (place, lax.all_gather(left_grad, "xl", axis=0, tiled=False), squares, right),
        flops,
    )
    sums, part = call(
        pair_sums_kernel,
        (shape((Y, 8, 128), f32),),
        (place, lax.all_gather(sums, "xl", axis=0, tiled=False)),
        through=part,
    )
    part_other = swap(part)
    sums = lax.all_to_all(sums, "y", split_axis=0, concat_axis=0, tiled=True)

    both, new_master, new_momentum = call(
        update_kernel,
        (shape((2, 2 * rows, width), bf16), shape(master.shape, f32), shape(master.shape, f32)),
        (place, sums, part, part_other, base, swapped, master, momentum),
        scratch_shapes=[pltpu.VMEM((2 * rows, width), f32)],
    )

    params = jnp.zeros((2, Y, 2 * rows, width), bf16)

    def put(params, chunk, block, distance):
        at = lax.rem(place[0] + distance + Y, Y)
        return lax.dynamic_update_slice(params, chunk[:, None], (block, at, 0, 0))

    params = put(params, both, 0, 0)
    up = down = both
    for step in range(1, 4):
        up, down = hop(up, 1), hop(down, -1)
        params = put(params, up, 0, -step)
        params = put(params, down, 0, step)
    params = put(params, hop(up[:1], 1), 0, 4)
    params = put(params, hop(down[1:], -1), 1, 4)
    params = params.reshape(2, 2 * Y * rows, width)
    return (params, new_master, new_momentum, new_second)


def solution(mesh):
    split = Mesh(mesh.devices.reshape(8, 2, 2, 8, 2), OWNERS + GROUP)
    state = P(OWNERS, GROUP, None)
    return jax.shard_map(
        on_device,
        mesh=split,
        in_specs=(P(None, GROUP + OWNERS, None),) + (state,) * 5,
        out_specs=(P(OWNERS, None, None), state, state, state),
        check_vma=False,
    )
```

```python
import jax
import jax.numpy as jnp
from jax import lax
from jax.experimental import pallas as pl
from jax.experimental.pallas import tpu as pltpu
from jax.sharding import Mesh, PartitionSpec as P

momentum_decay = 0.9
second_decay = 0.95
learn_rate = 0.05
adam_eps = 1e-08
norm_eps = 1e-06

Y = 8
OWNERS = ("z", "xh", "c")
GROUP = ("y", "xl")
SWAP = [(0, 1), (1, 0)]
VMEM = pl.BlockSpec(memory_space=pltpu.VMEM)
SMEM = pl.BlockSpec(memory_space=pltpu.SMEM)
ANY = pl.BlockSpec(memory_space=pl.ANY)
PARAMS = pltpu.CompilerParams(vmem_limit_bytes=12 * 1024 * 1024)


def swap(x):
    return lax.ppermute(x, "xl", SWAP)


def hop(x, way):
    return lax.ppermute(x, "y", [(i, (i + way) % Y) for i in range(Y)])


def adam_kernel(place, mine, theirs, second, *refs):
    new_second, squares = refs[-2:]
    rows = second.shape[1]
    half = place[1]
    ours = mine[pl.ds(pl.multiple_of(half * rows, rows), rows), :]
    others = theirs[pl.ds(pl.multiple_of(half * rows, rows), rows), :]
    for block in range(2):
        grad = jnp.where(half == block, ours, others).astype(jnp.float32)
        moment = second_decay * second[block] + (1.0 - second_decay) * grad * grad
        new_second[block] = moment
        step = grad / (jnp.sqrt(moment) + adam_eps)
        squares[block] = jnp.full(squares.shape[1:], jnp.sum(step * step), jnp.float32)


def left_products(distances, place, left_own, swapped, chunks, total):
    rows = left_own.shape[1]
    depth = chunks[0].shape[0]
    half = place[1]
    for distance, chunk in zip(distances, chunks):
        at = pl.multiple_of(lax.rem(place[0] + distance + Y, Y) * depth, depth)
        columns = jnp.concatenate(
            [left_own[half, :, pl.ds(at, depth)], swapped[:rows, pl.ds(at, depth)]], axis=0
        )
        part = jnp.dot(columns, chunk[...], preferred_element_type=jnp.float32)
        total = part if total is None else total + part
    return total


def early_kernel(distances, place, left_own, swapped, *refs):
    out = refs[len(distances)]
    out[...] = left_products(distances, place, left_own, swapped, refs[: len(distances)], None)


def late_kernel(distances, place, left_own, swapped, early, *refs):
    out = refs[-1]
    rows = left_own.shape[1]
    half = place[1]
    total = left_products(distances, place, left_own, swapped, refs[: len(distances)], early[...])
    rounded = total.astype(jnp.bfloat16)
    out[pl.ds(pl.multiple_of(half * rows, rows), rows), :] = rounded[:rows]
    out[pl.ds(pl.multiple_of((1 - half) * rows, rows), rows), :] = rounded[rows:]


def right_kernel(place, left_grads, adam, right, out, sums):
    depth = right.shape[0] * right.shape[2]
    squares = []
    for block in range(2):
        columns = right[:, block].reshape(depth, right.shape[3])
        part = lax.dot_general(
            left_grads[block], columns, (((1,), (1,)), ((), ())), preferred_element_type=jnp.float32
        )
        out[block] = part.astype(jnp.bfloat16)
        squares.append(jnp.sum(part * part))
    row = lax.broadcasted_iota(jnp.int32, (8, 128), 0)
    values = jnp.where(
        row < 2, jnp.where(row == 0, squares[0], squares[1]), jnp.where(row == 2, adam[0][:1], adam[1][:1])
    )
    for i in range(sums.shape[0]):
        sums[i] = values


def grafted(place, sums, mine, theirs, block, precond):
    half = place[1]
    total = jnp.sum(sums[...], axis=0)
    graft = jnp.sqrt(total[2 + block : 3 + block] / (total[block : block + 1] + norm_eps))
    low = lax.broadcasted_iota(jnp.int32, (precond.shape[0], 128), 1) < 64
    for i in range(Y // 2):
        cut = slice(i * 128, (i + 1) * 128)
        a = mine[block, :, cut].astype(jnp.float32)
        b = theirs[block, :, cut].astype(jnp.float32)
        first = jnp.where(half == 0, a, b)
        second = jnp.where(half == 0, b, a)
        even = jnp.where(low, first, pltpu.roll(second, 64, 1))
        odd = jnp.where(low, pltpu.roll(first, 64, 1), second)
        precond[:, 2 * i * 128 : (2 * i + 1) * 128] = graft * even
        precond[:, (2 * i + 1) * 128 : (2 * i + 2) * 128] = graft * odd


def params_kernel(place, sums, mine, theirs, base, swapped, params, precond):
    rows = base.shape[1]
    own = pl.ds(pl.multiple_of(place[1] * rows, rows), rows)
    other = pl.ds(pl.multiple_of((1 - place[1]) * rows, rows), rows)
    for block in range(2):
        grafted(place, sums, mine, theirs, block, precond)
        params[block, own, :] = (base[block] - learn_rate * precond[own, :]).astype(jnp.bfloat16)
        high = swapped[(1 + block) * rows : (2 + block) * rows, :].astype(jnp.float32)
        low = swapped[(3 + block) * rows : (4 + block) * rows, :].astype(jnp.float32)
        params[block, other, :] = (high + low - learn_rate * precond[other, :]).astype(jnp.bfloat16)


def state_kernel(place, sums, mine, theirs, master, momentum, both, new_master, new_momentum, params, precond):
    rows = master.shape[1]
    own = pl.ds(pl.multiple_of(place[1] * rows, rows), rows)
    for block in range(2):
        params[block, place[0]] = both[block]
        grafted(place, sums, mine, theirs, block, precond)
        moved = momentum_decay * momentum[block] + precond[own, :]
        new_momentum[block] = moved
        new_master[block] = master[block] - learn_rate * moved


def call(kernel, out_shape, operands, flops=0, ready=(), through=None, scratch_shapes=()):
    moved = sum(x.size * x.dtype.itemsize for x in operands)
    in_specs = [SMEM] + [VMEM] * (len(operands) - 1) + [ANY] * len(ready)
    operands, out_shape = tuple(operands) + tuple(ready), tuple(out_shape)
    out_specs = [VMEM] * len(out_shape)
    aliases = {}
    if through is not None:
        aliases = {len(operands): len(out_shape)}
        operands += (through,)
        out_shape += (jax.ShapeDtypeStruct(through.shape, through.dtype),)
        in_specs.append(ANY)
        out_specs.append(ANY)
    return pl.pallas_call(
        kernel,
        out_shape=out_shape,
        in_specs=in_specs,
        out_specs=tuple(out_specs),
        scratch_shapes=scratch_shapes,
        input_output_aliases=aliases,
        compiler_params=PARAMS,
        cost_estimate=pl.CostEstimate(flops=flops, bytes_accessed=2 * moved, transcendentals=0),
    )(*operands)


def on_device(grad, left_root, right_root, master, momentum, second):
    place = jnp.stack([lax.axis_index("y"), lax.axis_index("xl")])
    _, rows, width = master.shape
    shape = jax.ShapeDtypeStruct
    f32, bf16 = jnp.float32, jnp.bfloat16

    right = lax.all_gather(right_root, "y", axis=0, tiled=False)

    value = master - (learn_rate * momentum_decay) * momentum
    high = value.astype(bf16)
    low = (value - high.astype(f32)).astype(bf16)
    base = high.astype(f32) + low.astype(f32)
    left_away = jnp.where(place[1] == 0, left_root[1], left_root[0])
    swapped = swap(jnp.concatenate([left_away[None], high, low]).reshape(5 * rows, width))

    spread = lax.all_to_all(grad, OWNERS + ("xl",), split_axis=0, concat_axis=1, tiled=True)
    pair = spread.reshape(-1, 2, grad.shape[1], width).swapaxes(0, 1).reshape(2 * rows, width)

    up1, down1 = hop(pair, 1), hop(pair, -1)
    up2, down2 = hop(up1, 1), hop(down1, -1)
    up3, down3 = hop(up2, 1), hop(down2, -1)
    up4 = hop(up3, 1)
    new_second, squares = call(
        adam_kernel,
        (shape(second.shape, f32), shape((2, 8, 128), f32)),
        (place, pair, swap(pair), second),
        ready=(right[0, 0, :16, :128],),
    )

    flops = 4 * rows * width * width
    (early,) = call(
        lambda *refs: early_kernel((0, -1, 1, -2, 2, -3), *refs),
        (shape((2 * rows, width), f32),),
        (place, left_root, swapped, pair, up1, down1, up2, down2, up3),
        flops,
    )
    (left_grad,) = call(
        lambda *refs: late_kernel((3, -4), *refs),
        (shape((2 * rows, width), bf16),),
        (place, left_root, swapped, early, down3, up4),
        flops,
        ready=(squares,),
    )
    part, sums = call(
        right_kernel,
        (shape((2, 2 * rows, width // 2), bf16), shape((2 * Y, 8, 128), f32)),
        (place, lax.all_gather(left_grad, "xl", axis=0, tiled=False), squares, right),
        flops,
    )
    part_other = swap(part)
    sums = lax.all_to_all(sums, GROUP, split_axis=0, concat_axis=0, tiled=True)

    scratch = [pltpu.VMEM((2 * rows, width), f32)]
    (both,) = call(
        params_kernel,
        (shape((2, 2 * rows, width), bf16),),
        (place, sums, part, part_other, base, swapped),
        scratch_shapes=scratch,
    )
    new_master, new_momentum, params = call(
        state_kernel,
        (shape(master.shape, f32), shape(master.shape, f32), shape((2, Y, 2 * rows, width), bf16)),
        (place, sums, part, part_other, master, momentum, both),
        scratch_shapes=scratch,
    )

    def put(params, chunk, block, distance, row=0):
        at = lax.rem(place[0] + distance + Y, Y)
        return lax.dynamic_update_slice(params, chunk[:, None], (block, at, row, 0))

    up = down = both
    for step in range(1, 4):
        up, down = hop(up, 1), hop(down, -1)
        params = put(params, up, 0, -step)
        params = put(params, down, 0, step)
    up = hop(up.reshape(4, rows, width)[:3], 1)
    down = hop(down.reshape(4, rows, width)[3:], -1)
    params = put(params, up[:2].reshape(1, 2 * rows, width), 0, 4)
    params = put(params, up[2:], 1, 4)
    params = put(params, down, 1, 4, rows)
    params = params.reshape(2, 2 * Y * rows, width)
    return (params, new_master, new_momentum, new_second)


def solution(mesh):
    split = Mesh(mesh.devices.reshape(8, 2, 2, 8, 2), OWNERS + GROUP)
    state = P(OWNERS, GROUP, None)
    return jax.shard_map(
        on_device,
        mesh=split,
        in_specs=(P(None, GROUP + OWNERS, None),) + (state,) * 5,
        out_specs=(P(OWNERS, None, None), state, state, state),
        check_vma=False,
    )
```

```python
import jax
import jax.numpy as jnp
from jax import lax
from jax.experimental import pallas as pl
from jax.experimental.pallas import tpu as pltpu
from jax.sharding import Mesh, PartitionSpec as P

momentum_decay = 0.9
second_decay = 0.95
learn_rate = 0.05
adam_eps = 1e-08
norm_eps = 1e-06

Y = 8
OWNERS = ("z", "xh", "c")
GROUP = ("y", "xl")
SWAP = [(0, 1), (1, 0)]
VMEM = pl.BlockSpec(memory_space=pltpu.VMEM)
SMEM = pl.BlockSpec(memory_space=pltpu.SMEM)
ANY = pl.BlockSpec(memory_space=pl.ANY)
PARAMS = pltpu.CompilerParams(vmem_limit_bytes=12 * 1024 * 1024)


def swap(x):
    return lax.ppermute(x, "xl", SWAP)


def hop(x, way):
    return lax.ppermute(x, "y", [(i, (i + way) % Y) for i in range(Y)])


def adam_kernel(place, mine, swapped, second, *refs):
    new_second, squares = refs[-2:]
    rows = second.shape[1]
    half = place[1]
    ours = mine[pl.ds(pl.multiple_of(half * rows, rows), rows), :]
    others = swapped[5 * rows :, :]
    for block in range(2):
        grad = jnp.where(half == block, ours, others).astype(jnp.float32)
        moment = second_decay * second[block] + (1.0 - second_decay) * grad * grad
        new_second[block] = moment
        step = grad / (jnp.sqrt(moment) + adam_eps)
        squares[block] = jnp.full(squares.shape[1:], jnp.sum(step * step), jnp.float32)


def left_products(distances, place, left_own, swapped, chunks, total):
    rows = left_own.shape[1]
    depth = chunks[0].shape[0]
    half = place[1]
    for distance, chunk in zip(distances, chunks):
        at = pl.multiple_of(lax.rem(place[0] + distance + Y, Y) * depth, depth)
        columns = jnp.concatenate(
            [left_own[half, :, pl.ds(at, depth)], swapped[:rows, pl.ds(at, depth)]], axis=0
        )
        part = jnp.dot(columns, chunk[...], preferred_element_type=jnp.float32)
        total = part if total is None else total + part
    return total


def early_kernel(distances, place, left_own, swapped, *refs):
    out = refs[len(distances)]
    out[...] = left_products(distances, place, left_own, swapped, refs[: len(distances)], None)


def late_kernel(distances, place, left_own, swapped, early, *refs):
    out = refs[-1]
    rows = left_own.shape[1]
    half = place[1]
    total = left_products(distances, place, left_own, swapped, refs[: len(distances)], early[...])
    rounded = total.astype(jnp.bfloat16)
    out[pl.ds(pl.multiple_of(half * rows, rows), rows), :] = rounded[:rows]
    out[pl.ds(pl.multiple_of((1 - half) * rows, rows), rows), :] = rounded[rows:]


def right_kernel(place, left_grads, adam, right, out, sums):
    depth = right.shape[0] * right.shape[2]
    squares = []
    for block in range(2):
        columns = right[:, block].reshape(depth, right.shape[3])
        part = lax.dot_general(
            left_grads[block], columns, (((1,), (1,)), ((), ())), preferred_element_type=jnp.float32
        )
        out[block] = part.astype(jnp.bfloat16)
        squares.append(jnp.sum(part * part))
    row = lax.broadcasted_iota(jnp.int32, (8, 128), 0)
    values = jnp.where(
        row < 2, jnp.where(row == 0, squares[0], squares[1]), jnp.where(row == 2, adam[0][:1], adam[1][:1])
    )
    for i in range(sums.shape[0]):
        sums[i] = values


def grafted(place, sums, mine, theirs, block, precond):
    half = place[1]
    total = jnp.sum(sums[...], axis=0)
    graft = jnp.sqrt(total[2 + block : 3 + block] / (total[block : block + 1] + norm_eps))
    low = lax.broadcasted_iota(jnp.int32, (precond.shape[0], 128), 1) < 64
    for i in range(Y // 2):
        cut = slice(i * 128, (i + 1) * 128)
        a = mine[block, :, cut].astype(jnp.float32)
        b = theirs[block, :, cut].astype(jnp.float32)
        first = jnp.where(half == 0, a, b)
        second = jnp.where(half == 0, b, a)
        even = jnp.where(low, first, pltpu.roll(second, 64, 1))
        odd = jnp.where(low, pltpu.roll(first, 64, 1), second)
        precond[:, 2 * i * 128 : (2 * i + 1) * 128] = graft * even
        precond[:, (2 * i + 1) * 128 : (2 * i + 2) * 128] = graft * odd


def params_kernel(place, sums, mine, theirs, base, swapped, params, precond):
    rows = base.shape[1]
    own = pl.ds(pl.multiple_of(place[1] * rows, rows), rows)
    other = pl.ds(pl.multiple_of((1 - place[1]) * rows, rows), rows)
    for block in range(2):
        grafted(place, sums, mine, theirs, block, precond)
        params[block, own, :] = (base[block] - learn_rate * precond[own, :]).astype(jnp.bfloat16)
        high = swapped[(1 + block) * rows : (2 + block) * rows, :].astype(jnp.float32)
        low = swapped[(3 + block) * rows : (4 + block) * rows, :].astype(jnp.float32)
        params[block, other, :] = (high + low - learn_rate * precond[other, :]).astype(jnp.bfloat16)


def state_kernel(place, sums, mine, theirs, master, momentum, both, new_master, new_momentum, params, precond):
    rows = master.shape[1]
    own = pl.ds(pl.multiple_of(place[1] * rows, rows), rows)
    for block in range(2):
        params[block, place[0]] = both[block]
        grafted(place, sums, mine, theirs, block, precond)
        moved = momentum_decay * momentum[block] + precond[own, :]
        new_momentum[block] = moved
        new_master[block] = master[block] - learn_rate * moved


def call(kernel, out_shape, operands, flops=0, ready=(), through=None, scratch_shapes=()):
    moved = sum(x.size * x.dtype.itemsize for x in operands)
    in_specs = [SMEM] + [VMEM] * (len(operands) - 1) + [ANY] * len(ready)
    operands, out_shape = tuple(operands) + tuple(ready), tuple(out_shape)
    out_specs = [VMEM] * len(out_shape)
    aliases = {}
    if through is not None:
        aliases = {len(operands): len(out_shape)}
        operands += (through,)
        out_shape += (jax.ShapeDtypeStruct(through.shape, through.dtype),)
        in_specs.append(ANY)
        out_specs.append(ANY)
    return pl.pallas_call(
        kernel,
        out_shape=out_shape,
        in_specs=in_specs,
        out_specs=tuple(out_specs),
        scratch_shapes=scratch_shapes,
        input_output_aliases=aliases,
        compiler_params=PARAMS,
        cost_estimate=pl.CostEstimate(flops=flops, bytes_accessed=2 * moved, transcendentals=0),
    )(*operands)


def later(place, x, *ready):
    return call(lambda *refs: None, (), (place,), ready=ready, through=x)[0]


def on_device(grad, left_root, right_root, master, momentum, second):
    place = jnp.stack([lax.axis_index("y"), lax.axis_index("xl")])
    _, rows, width = master.shape
    shape = jax.ShapeDtypeStruct
    f32, bf16 = jnp.float32, jnp.bfloat16

    right = lax.all_gather(right_root, "y", axis=0, tiled=False)

    value = master - (learn_rate * momentum_decay) * momentum
    high = value.astype(bf16)
    low = (value - high.astype(f32)).astype(bf16)
    base = high.astype(f32) + low.astype(f32)
    left_away = jnp.where(place[1] == 0, left_root[1], left_root[0])

    spread = lax.all_to_all(grad, OWNERS + ("xl",), split_axis=0, concat_axis=1, tiled=True)
    pair = spread.reshape(-1, 2, grad.shape[1], width).swapaxes(0, 1).reshape(2 * rows, width)

    pair = later(place, pair, left_away, high, low, base)
    up1, down1 = hop(pair, 1), hop(pair, -1)
    halves = pair.reshape(2, rows, width)
    pair_away = jnp.where(place[1] == 0, halves[1], halves[0])
    swapped = swap(jnp.concatenate([left_away[None], high, low, pair_away[None]]).reshape(6 * rows, width))
    up2, down2 = hop(up1, 1), hop(down1, -1)
    up3, down3 = hop(up2, 1), hop(down2, -1)
    up4 = hop(up3, 1)
    new_second, squares = call(
        adam_kernel,
        (shape(second.shape, f32), shape((2, 8, 128), f32)),
        (place, pair, swapped, second),
        ready=(right[0, 0, :16, :128],),
    )

    flops = 4 * rows * width * width
    (early,) = call(
        lambda *refs: early_kernel((0, -1, 1, -2, 2, -3), *refs),
        (shape((2 * rows, width), f32),),
        (place, left_root, swapped, pair, up1, down1, up2, down2, up3),
        flops,
    )
    (left_grad,) = call(
        lambda *refs: late_kernel((3, -4), *refs),
        (shape((2 * rows, width), bf16),),
        (place, left_root, swapped, early, down3, up4),
        flops,
        ready=(squares,),
    )
    part, sums = call(
        right_kernel,
        (shape((2, 2 * rows, width // 2), bf16), shape((2 * Y, 8, 128), f32)),
        (place, lax.all_gather(left_grad, "xl", axis=0, tiled=False), squares, right),
        flops,
    )
    part_other = swap(part)
    sums = lax.all_to_all(sums, GROUP, split_axis=0, concat_axis=0, tiled=True)

    scratch = [pltpu.VMEM((2 * rows, width), f32)]
    (both,) = call(
        params_kernel,
        (shape((2, 2 * rows, width), bf16),),
        (place, sums, part, part_other, base, swapped),
        scratch_shapes=scratch,
    )
    new_master, new_momentum, params = call(
        state_kernel,
        (shape(master.shape, f32), shape(master.shape, f32), shape((2, Y, 2 * rows, width), bf16)),
        (place, sums, part, part_other, master, momentum, both),
        scratch_shapes=scratch,
    )

    def put(params, chunk, block, distance, row=0):
        at = lax.rem(place[0] + distance + Y, Y)
        return lax.dynamic_update_slice(params, chunk[:, None], (block, at, row, 0))

    up = down = both
    for step in range(1, 4):
        up, down = hop(up, 1), hop(down, -1)
        params = put(params, up, 0, -step)
        params = put(params, down, 0, step)
    up = hop(up.reshape(4, rows, width)[:3], 1)
    down = hop(down.reshape(4, rows, width)[3:], -1)
    params = put(params, up[:2].reshape(1, 2 * rows, width), 0, 4)
    params = put(params, up[2:], 1, 4)
    params = put(params, down, 1, 4, rows)
    params = params.reshape(2, 2 * Y * rows, width)
    return (params, new_master, new_momentum, new_second)


def solution(mesh):
    split = Mesh(mesh.devices.reshape(8, 2, 2, 8, 2), OWNERS + GROUP)
    state = P(OWNERS, GROUP, None)
    return jax.shard_map(
        on_device,
        mesh=split,
        in_specs=(P(None, GROUP + OWNERS, None),) + (state,) * 5,
        out_specs=(P(OWNERS, None, None), state, state, state),
        check_vma=False,
    )
```

```python
import jax
import jax.numpy as jnp
from jax import lax
from jax.experimental import pallas as pl
from jax.experimental.pallas import tpu as pltpu
from jax.sharding import Mesh, PartitionSpec as P

momentum_decay = 0.9
second_decay = 0.95
learn_rate = 0.05
adam_eps = 1e-08
norm_eps = 1e-06

Y = 8
OWNERS = ("z", "xh", "c")
GROUP = ("y", "xl")
SWAP = [(0, 1), (1, 0)]
VMEM = pl.BlockSpec(memory_space=pltpu.VMEM)
SMEM = pl.BlockSpec(memory_space=pltpu.SMEM)
ANY = pl.BlockSpec(memory_space=pl.ANY)
PARAMS = pltpu.CompilerParams(vmem_limit_bytes=12 * 1024 * 1024)


def swap(x):
    return lax.ppermute(x, "xl", SWAP)


def hop(x, way):
    return lax.ppermute(x, "y", [(i, (i + way) % Y) for i in range(Y)])


def adam_kernel(place, mine, swapped, second, *refs):
    new_second, squares = refs[-2:]
    rows = second.shape[1]
    half = place[1]
    ours = mine[pl.ds(pl.multiple_of(half * rows, rows), rows), :]
    others = swapped[5 * rows :, :]
    for block in range(2):
        grad = jnp.where(half == block, ours, others).astype(jnp.float32)
        moment = second_decay * second[block] + (1.0 - second_decay) * grad * grad
        new_second[block] = moment
        step = grad / (jnp.sqrt(moment) + adam_eps)
        squares[block] = jnp.full(squares.shape[1:], jnp.sum(step * step), jnp.float32)


def left_products(distances, place, left_own, swapped, chunks, total):
    rows = left_own.shape[1]
    depth = chunks[0].shape[0]
    half = place[1]
    for distance, chunk in zip(distances, chunks):
        at = pl.multiple_of(lax.rem(place[0] + distance + Y, Y) * depth, depth)
        columns = jnp.concatenate(
            [left_own[half, :, pl.ds(at, depth)], swapped[:rows, pl.ds(at, depth)]], axis=0
        )
        part = jnp.dot(columns, chunk[...], preferred_element_type=jnp.float32)
        total = part if total is None else total + part
    return total


def early_kernel(distances, place, left_own, swapped, *refs):
    out = refs[len(distances)]
    out[...] = left_products(distances, place, left_own, swapped, refs[: len(distances)], None)


def late_kernel(distances, place, left_own, swapped, early, *refs):
    out = refs[-1]
    rows = left_own.shape[1]
    half = place[1]
    total = left_products(distances, place, left_own, swapped, refs[: len(distances)], early[...])
    rounded = total.astype(jnp.bfloat16)
    out[pl.ds(pl.multiple_of(half * rows, rows), rows), :] = rounded[:rows]
    out[pl.ds(pl.multiple_of((1 - half) * rows, rows), rows), :] = rounded[rows:]


def right_kernel(place, left_grads, adam, right, out, sums):
    depth = right.shape[0] * right.shape[2]
    squares = []
    for block in range(2):
        columns = right[:, block].reshape(depth, right.shape[3])
        part = lax.dot_general(
            left_grads[block], columns, (((1,), (1,)), ((), ())), preferred_element_type=jnp.float32
        )
        out[block] = part.astype(jnp.bfloat16)
        squares.append(jnp.sum(part * part))
    lane = lax.broadcasted_iota(jnp.int32, (1, 128), 1)
    values = jnp.where(
        lane < 2, jnp.where(lane == 0, squares[0], squares[1]), jnp.where(lane == 2, adam[0][:1], adam[1][:1])
    )
    for i in range(sums.shape[0]):
        sums[i] = values


def grafted(place, sums, mine, theirs, block, precond):
    half = place[1]
    total = jnp.sum(sums[...], axis=0)
    lane = lax.broadcasted_iota(jnp.int32, total.shape, 1)

    def spread(i):
        return jnp.full(total.shape, jnp.sum(jnp.where(lane == i, total, 0.0)), jnp.float32)

    graft = jnp.sqrt(spread(2 + block) / (spread(block) + norm_eps))
    low = lax.broadcasted_iota(jnp.int32, (precond.shape[0], 128), 1) < 64
    for i in range(Y // 2):
        cut = slice(i * 128, (i + 1) * 128)
        a = mine[block, :, cut].astype(jnp.float32)
        b = theirs[block, :, cut].astype(jnp.float32)
        first = jnp.where(half == 0, a, b)
        second = jnp.where(half == 0, b, a)
        even = jnp.where(low, first, pltpu.roll(second, 64, 1))
        odd = jnp.where(low, pltpu.roll(first, 64, 1), second)
        precond[:, 2 * i * 128 : (2 * i + 1) * 128] = graft * even
        precond[:, (2 * i + 1) * 128 : (2 * i + 2) * 128] = graft * odd


def params_kernel(place, sums, mine, theirs, base, swapped, params, precond):
    rows = base.shape[1]
    own = pl.ds(pl.multiple_of(place[1] * rows, rows), rows)
    other = pl.ds(pl.multiple_of((1 - place[1]) * rows, rows), rows)
    for block in range(2):
        grafted(place, sums, mine, theirs, block, precond)
        params[block, own, :] = (base[block] - learn_rate * precond[own, :]).astype(jnp.bfloat16)
        high = swapped[(1 + block) * rows : (2 + block) * rows, :].astype(jnp.float32)
        low = swapped[(3 + block) * rows : (4 + block) * rows, :].astype(jnp.float32)
        params[block, other, :] = (high + low - learn_rate * precond[other, :]).astype(jnp.bfloat16)


def state_kernel(place, sums, mine, theirs, master, momentum, both, new_master, new_momentum, params, precond):
    rows = master.shape[1]
    own = pl.ds(pl.multiple_of(place[1] * rows, rows), rows)
    for block in range(2):
        params[block, place[0]] = both[block]
        grafted(place, sums, mine, theirs, block, precond)
        moved = momentum_decay * momentum[block] + precond[own, :]
        new_momentum[block] = moved
        new_master[block] = master[block] - learn_rate * moved


def call(kernel, out_shape, operands, flops=0, ready=(), through=None, scratch_shapes=()):
    moved = sum(x.size * x.dtype.itemsize for x in operands)
    in_specs = [SMEM] + [VMEM] * (len(operands) - 1) + [ANY] * len(ready)
    operands, out_shape = tuple(operands) + tuple(ready), tuple(out_shape)
    out_specs = [VMEM] * len(out_shape)
    aliases = {}
    if through is not None:
        aliases = {len(operands): len(out_shape)}
        operands += (through,)
        out_shape += (jax.ShapeDtypeStruct(through.shape, through.dtype),)
        in_specs.append(ANY)
        out_specs.append(ANY)
    return pl.pallas_call(
        kernel,
        out_shape=out_shape,
        in_specs=in_specs,
        out_specs=tuple(out_specs),
        scratch_shapes=scratch_shapes,
        input_output_aliases=aliases,
        compiler_params=PARAMS,
        cost_estimate=pl.CostEstimate(flops=flops, bytes_accessed=2 * moved, transcendentals=0),
    )(*operands)


def later(place, x, *ready):
    return call(lambda *refs: None, (), (place,), ready=ready, through=x)[0]


def on_device(grad, left_root, right_root, master, momentum, second):
    place = jnp.stack([lax.axis_index("y"), lax.axis_index("xl")])
    _, rows, width = master.shape
    shape = jax.ShapeDtypeStruct
    f32, bf16 = jnp.float32, jnp.bfloat16

    right = lax.all_gather(right_root, "y", axis=0, tiled=False)

    value = master - (learn_rate * momentum_decay) * momentum
    high = value.astype(bf16)
    low = (value - high.astype(f32)).astype(bf16)
    base = high.astype(f32) + low.astype(f32)
    left_away = jnp.where(place[1] == 0, left_root[1], left_root[0])

    spread = lax.all_to_all(grad, OWNERS + ("xl",), split_axis=0, concat_axis=1, tiled=True)
    pair = spread.reshape(-1, 2, grad.shape[1], width).swapaxes(0, 1).reshape(2 * rows, width)

    pair = later(place, pair, left_away, high, low, base)
    up1, down1 = hop(pair, 1), hop(pair, -1)
    halves = pair.reshape(2, rows, width)
    pair_away = jnp.where(place[1] == 0, halves[1], halves[0])
    swapped = swap(jnp.concatenate([left_away[None], high, low, pair_away[None]]).reshape(6 * rows, width))
    up2, down2 = hop(up1, 1), hop(down1, -1)
    up3, down3 = hop(up2, 1), hop(down2, -1)
    up4 = hop(up3, 1)
    new_second, squares = call(
        adam_kernel,
        (shape(second.shape, f32), shape((2, 8, 128), f32)),
        (place, pair, swapped, second),
        ready=(right[0, 0, :16, :128],),
    )

    flops = 4 * rows * width * width
    (early,) = call(
        lambda *refs: early_kernel((0, -1, 1, -2, 2, -3), *refs),
        (shape((2 * rows, width), f32),),
        (place, left_root, swapped, pair, up1, down1, up2, down2, up3),
        flops,
    )
    (left_grad,) = call(
        lambda *refs: late_kernel((3, -4), *refs),
        (shape((2 * rows, width), bf16),),
        (place, left_root, swapped, early, down3, up4),
        flops,
        ready=(squares,),
    )
    part, sums = call(
        right_kernel,
        (shape((2, 2 * rows, width // 2), bf16), shape((2 * Y, 1, 128), f32)),
        (place, lax.all_gather(left_grad, "xl", axis=0, tiled=False), squares, right),
        flops,
    )
    part_other = swap(part)
    sums = lax.all_to_all(sums, GROUP, split_axis=0, concat_axis=0, tiled=True)

    scratch = [pltpu.VMEM((2 * rows, width), f32)]
    (both,) = call(
        params_kernel,
        (shape((2, 2 * rows, width), bf16),),
        (place, sums, part, part_other, base, swapped),
        scratch_shapes=scratch,
    )
    new_master, new_momentum, params = call(
        state_kernel,
        (shape(master.shape, f32), shape(master.shape, f32), shape((2, Y, 2 * rows, width), bf16)),
        (place, sums, part, part_other, master, momentum, both),
        scratch_shapes=scratch,
    )

    def put(params, chunk, block, distance):
        at = lax.rem(place[0] + distance + Y, Y)
        return lax.dynamic_update_slice(params, chunk[:, None], (block, at, 0, 0))

    up = down = both
    for step in range(1, 4):
        up, down = hop(up, 1), hop(down, -1)
        params = put(params, up, 0, -step)
        params = put(params, down, 0, step)
    for block in range(2):
        params = put(params, hop(up[block : block + 1], 1), block, 4)
    params = params.reshape(2, 2 * Y * rows, width)
    return (params, new_master, new_momentum, new_second)


def solution(mesh):
    split = Mesh(mesh.devices.reshape(8, 2, 2, 8, 2), OWNERS + GROUP)
    state = P(OWNERS, GROUP, None)
    return jax.shard_map(
        on_device,
        mesh=split,
        in_specs=(P(None, GROUP + OWNERS, None),) + (state,) * 5,
        out_specs=(P(OWNERS, None, None), state, state, state),
        check_vma=False,
    )
```

```python
import jax
import jax.numpy as jnp
from jax import lax
from jax.experimental import pallas as pl
from jax.experimental.pallas import tpu as pltpu
from jax.sharding import Mesh, PartitionSpec as P

momentum_decay = 0.9
second_decay = 0.95
learn_rate = 0.05
adam_eps = 1e-08
norm_eps = 1e-06

Y = 8
OWNERS = ("z", "xh", "c")
GROUP = ("y", "xl")
SWAP = [(0, 1), (1, 0)]
VMEM = pl.BlockSpec(memory_space=pltpu.VMEM)
SMEM = pl.BlockSpec(memory_space=pltpu.SMEM)
ANY = pl.BlockSpec(memory_space=pl.ANY)
PARAMS = pltpu.CompilerParams(vmem_limit_bytes=12 * 1024 * 1024)


def swap(x):
    return lax.ppermute(x, "xl", SWAP)


def hop(x, way):
    return lax.ppermute(x, "y", [(i, (i + way) % Y) for i in range(Y)])


def adam_kernel(place, mine, swapped, second, *refs):
    new_second, squares = refs[-2:]
    rows = second.shape[1]
    half = place[1]
    ours = mine[pl.ds(pl.multiple_of(half * rows, rows), rows), :]
    others = swapped[5 * rows :, :]
    for block in range(2):
        grad = jnp.where(half == block, ours, others).astype(jnp.float32)
        moment = second_decay * second[block] + (1.0 - second_decay) * grad * grad
        new_second[block] = moment
        step = grad / (jnp.sqrt(moment) + adam_eps)
        squares[block] = jnp.full(squares.shape[1:], jnp.sum(step * step), jnp.float32)


def left_products(distances, place, left_own, swapped, chunks, total):
    rows = left_own.shape[1]
    depth = chunks[0].shape[0]
    half = place[1]
    for distance, chunk in zip(distances, chunks):
        at = pl.multiple_of(lax.rem(place[0] + distance + Y, Y) * depth, depth)
        columns = jnp.concatenate(
            [left_own[half, :, pl.ds(at, depth)], swapped[:rows, pl.ds(at, depth)]], axis=0
        )
        part = jnp.dot(columns, chunk[...], preferred_element_type=jnp.float32)
        total = part if total is None else total + part
    return total


def early_kernel(distances, place, left_own, swapped, *refs):
    out = refs[len(distances)]
    out[...] = left_products(distances, place, left_own, swapped, refs[: len(distances)], None)


def late_kernel(distances, place, left_own, swapped, early, *refs):
    out = refs[-1]
    rows = left_own.shape[1]
    half = place[1]
    total = left_products(distances, place, left_own, swapped, refs[: len(distances)], early[...])
    rounded = total.astype(jnp.bfloat16)
    out[pl.ds(pl.multiple_of(half * rows, rows), rows), :] = rounded[:rows]
    out[pl.ds(pl.multiple_of((1 - half) * rows, rows), rows), :] = rounded[rows:]


def right_kernel(place, left_grads, adam, right, out, sums):
    depth = right.shape[0] * right.shape[2]
    squares = []
    for block in range(2):
        columns = right[:, block].reshape(depth, right.shape[3])
        part = lax.dot_general(
            left_grads[block], columns, (((1,), (1,)), ((), ())), preferred_element_type=jnp.float32
        )
        out[block] = part.astype(jnp.bfloat16)
        squares.append(jnp.sum(part * part))
    lane = lax.broadcasted_iota(jnp.int32, (1, 128), 1)
    values = jnp.where(
        lane < 2, jnp.where(lane == 0, squares[0], squares[1]), jnp.where(lane == 2, adam[0][:1], adam[1][:1])
    )
    for i in range(sums.shape[0]):
        sums[i] = values


def grafted(place, sums, mine, theirs, block, precond):
    half = place[1]
    total = jnp.sum(sums[...], axis=0)
    lane = lax.broadcasted_iota(jnp.int32, total.shape, 1)

    def spread(i):
        return jnp.full(total.shape, jnp.sum(jnp.where(lane == i, total, 0.0)), jnp.float32)

    graft = jnp.sqrt(spread(2 + block) / (spread(block) + norm_eps))
    low = lax.broadcasted_iota(jnp.int32, (precond.shape[0], 128), 1) < 64
    for i in range(Y // 2):
        cut = slice(i * 128, (i + 1) * 128)
        a = mine[block, :, cut].astype(jnp.float32)
        b = theirs[block, :, cut].astype(jnp.float32)
        first = jnp.where(half == 0, a, b)
        second = jnp.where(half == 0, b, a)
        even = jnp.where(low, first, pltpu.roll(second, 64, 1))
        odd = jnp.where(low, pltpu.roll(first, 64, 1), second)
        precond[:, 2 * i * 128 : (2 * i + 1) * 128] = graft * even
        precond[:, (2 * i + 1) * 128 : (2 * i + 2) * 128] = graft * odd


def params_kernel(place, sums, mine, theirs, base, swapped, params, precond):
    rows = base.shape[1]
    own = pl.ds(pl.multiple_of(place[1] * rows, rows), rows)
    other = pl.ds(pl.multiple_of((1 - place[1]) * rows, rows), rows)
    for block in range(2):
        grafted(place, sums, mine, theirs, block, precond)
        params[block, own, :] = (base[block] - learn_rate * precond[own, :]).astype(jnp.bfloat16)
        high = swapped[(1 + block) * rows : (2 + block) * rows, :].astype(jnp.float32)
        low = swapped[(3 + block) * rows : (4 + block) * rows, :].astype(jnp.float32)
        params[block, other, :] = (high + low - learn_rate * precond[other, :]).astype(jnp.bfloat16)


def state_kernel(place, sums, mine, theirs, master, momentum, both, new_master, new_momentum, params, precond):
    rows = master.shape[1]
    own = pl.ds(pl.multiple_of(place[1] * rows, rows), rows)
    for block in range(2):
        params[block, place[0]] = both[block]
        grafted(place, sums, mine, theirs, block, precond)
        moved = momentum_decay * momentum[block] + precond[own, :]
        new_momentum[block] = moved
        new_master[block] = master[block] - learn_rate * moved


def call(kernel, out_shape, operands, flops=0, ready=(), through=None, scratch_shapes=()):
    moved = sum(x.size * x.dtype.itemsize for x in operands)
    in_specs = [SMEM] + [VMEM] * (len(operands) - 1) + [ANY] * len(ready)
    operands, out_shape = tuple(operands) + tuple(ready), tuple(out_shape)
    out_specs = [VMEM] * len(out_shape)
    aliases = {}
    if through is not None:
        aliases = {len(operands): len(out_shape)}
        operands += (through,)
        out_shape += (jax.ShapeDtypeStruct(through.shape, through.dtype),)
        in_specs.append(ANY)
        out_specs.append(ANY)
    return pl.pallas_call(
        kernel,
        out_shape=out_shape,
        in_specs=in_specs,
        out_specs=tuple(out_specs),
        scratch_shapes=scratch_shapes,
        input_output_aliases=aliases,
        compiler_params=PARAMS,
        cost_estimate=pl.CostEstimate(flops=flops, bytes_accessed=2 * moved, transcendentals=0),
    )(*operands)


def later(place, x, *ready):
    return call(lambda *refs: None, (), (place,), ready=ready, through=x)[0]


def on_device(grad, left_root, right_root, master, momentum, second):
    place = jnp.stack([lax.axis_index("y"), lax.axis_index("xl")])
    _, rows, width = master.shape
    shape = jax.ShapeDtypeStruct
    f32, bf16 = jnp.float32, jnp.bfloat16

    right = lax.all_gather(right_root, "y", axis=0, tiled=False)

    value = master - (learn_rate * momentum_decay) * momentum
    high = value.astype(bf16)
    low = (value - high.astype(f32)).astype(bf16)
    base = high.astype(f32) + low.astype(f32)
    left_away = jnp.where(place[1] == 0, left_root[1], left_root[0])

    spread = lax.all_to_all(grad, OWNERS + ("xl",), split_axis=0, concat_axis=1, tiled=True)
    pair = spread.reshape(-1, 2, grad.shape[1], width).swapaxes(0, 1).reshape(2 * rows, width)

    pair = later(place, pair, left_away, high, low, base)
    up1, down1 = hop(pair, 1), hop(pair, -1)
    halves = pair.reshape(2, rows, width)
    pair_away = jnp.where(place[1] == 0, halves[1], halves[0])
    swapped = swap(jnp.concatenate([left_away[None], high, low, pair_away[None]]).reshape(6 * rows, width))
    up2, down2 = hop(up1, 1), hop(down1, -1)
    up3, down3 = hop(up2, 1), hop(down2, -1)
    up4 = hop(up3, 1)
    new_second, squares = call(
        adam_kernel,
        (shape(second.shape, f32), shape((2, 8, 128), f32)),
        (place, pair, swapped, second),
        ready=(right[0, 0, :16, :128],),
    )

    flops = 4 * rows * width * width
    (early,) = call(
        lambda *refs: early_kernel((0, -1, 1, -2, 2, -3), *refs),
        (shape((2 * rows, width), f32),),
        (place, left_root, swapped, pair, up1, down1, up2, down2, up3),
        flops,
    )
    (left_grad,) = call(
        lambda *refs: late_kernel((3, -4), *refs),
        (shape((2 * rows, width), bf16),),
        (place, left_root, swapped, early, down3, up4),
        flops,
        ready=(squares,),
    )
    part, sums = call(
        right_kernel,
        (shape((2, 2 * rows, width // 2), bf16), shape((2 * Y, 1, 128), f32)),
        (place, lax.all_gather(left_grad, "xl", axis=0, tiled=False), squares, right),
        flops,
    )
    part_other = swap(part)
    sums = lax.all_to_all(sums, GROUP, split_axis=0, concat_axis=0, tiled=True)

    scratch = [pltpu.VMEM((2 * rows, width), f32)]
    (both,) = call(
        params_kernel,
        (shape((2, 2 * rows, width), bf16),),
        (place, sums, part, part_other, base, swapped),
        scratch_shapes=scratch,
    )
    new_master, new_momentum, params = call(
        state_kernel,
        (shape(master.shape, f32), shape(master.shape, f32), shape((2, Y, 2 * rows, width), bf16)),
        (place, sums, part, part_other, master, momentum, both),
        scratch_shapes=scratch,
    )

    def put(params, chunk, block, distance):
        at = lax.rem(place[0] + distance + Y, Y)
        return lax.dynamic_update_slice(params, chunk[:, None], (block, at, 0, 0))

    ups, down = [both[:1], both[1:]], both
    for step in range(1, 5):
        ups = [hop(up, 1) for up in ups]
        if step < 4:
            down = hop(down, -1)
            params = put(params, down, 0, step)
        for block in range(2):
            params = put(params, ups[block], block, -step)
    params = params.reshape(2, 2 * Y * rows, width)
    return (params, new_master, new_momentum, new_second)


def solution(mesh):
    split = Mesh(mesh.devices.reshape(8, 2, 2, 8, 2), OWNERS + GROUP)
    state = P(OWNERS, GROUP, None)
    return jax.shard_map(
        on_device,
        mesh=split,
        in_specs=(P(None, GROUP + OWNERS, None),) + (state,) * 5,
        out_specs=(P(OWNERS, None, None), state, state, state),
        check_vma=False,
    )
```
